32 devices in a mesh: rep: 1, expert: 32 (over z, y, x, core), fsdp: 1.
Axes of the slice: x: 2, y: 2, z: 4, core: 2. Of those that a mesh axis runs over, the one named last changes fastest.
Arguments:
- tokens: bfloat16 [512, 3584], P(('rep', 'expert', 'fsdp')), may hold values from -6 to 6
- expert_ids: int32 [512, 8], P(('rep', 'expert', 'fsdp')), may hold values from 0 to 31, all different within a row; in each aligned block of 16 rows (0 to 15, 16 to 31, ...) at most 8 rows name the same one
- gate_logits: float32 [512, 8], P(('rep', 'expert', 'fsdp')), may hold values from -6 to 6
- bin_ids: int32 [512, 8, 8], P(('rep', 'expert', 'fsdp')), may hold values from 0 to 2047
- up_weight: bfloat16 [32, 3584, 1024], P('expert', 'fsdp'), may hold values from -0.09375 to 0.09375
Outputs:
- mixed: bfloat16 [512, 1024], P(('rep', 'expert', 'fsdp'))
- histogram: float32 [32, 8, 2048], P(('rep', 'expert'), None, 'fsdp')
The draws below stay inside these ranges and needn't reach their ends.
Inputs may be any that keep to these rules, and one draw needn't show every extreme that they name: `expert_ids`: each token names 8 different experts; among the tokens of one device no expert is named by more than 8 of them, a bound that some block reaches.
All inputs are finite; a program needn't handle non-finite values.
Results may differ from the reference program's by a relative error of at most 0.015.
Values may be sent and summed in bfloat16 or wider, within the bound.
No kernel may reach another device: no remote copies, remote signals or barrier semaphores. Data moves between devices by JAX's collectives and lax.ppermute only.
A program may use at most 64 MiB of HBM per device.

```python
import math
import jax
import jax.numpy as jnp
import numpy as np
from jax import lax

D = 3584
H = 1024
TOP = 8
BLOCK = 128
NBINS = 2048
TOK_DEV = 16
EXPERTS = 32
MOST = 8
BLOCKS = 8
TOKENS = 512
N_EXPERT = 32
N_FSDP = 1


def plant(result, stream_key, least, high):
    extent = result.shape
    spot = [jax.random.randint(jax.random.fold_in(stream_key, axis), (), 0, extent[axis]) for axis in range(len(extent))]
    result = result.at[tuple(spot)].set(least)
    longest = extent.index(max(extent))
    spot[longest] = (spot[longest] + 1) % extent[longest]
    return result.at[tuple(spot)].set(high)


def shard_levels(own_key, dims, shards, low, high):
    def one(position, shards_of):
        steps = jax.random.uniform(jax.random.fold_in(jax.random.fold_in(own_key, 6), position), (shards_of,), jnp.float32, low / len(shards), high / len(shards))
        return jnp.repeat(jnp.exp(steps), dims[position] // shards_of).reshape((-1,) + (1,) * (len(dims) - position - 1))

    factor_of = one(*shards[0])
    for cut in shards[1:]:
        factor_of = factor_of * one(*cut)
    return factor_of


def cumulative_ranks(amount, lean):
    loads = [(1 << 20) // math.isqrt(rank ** lean) + 1 for rank in range(1, amount + 1)]
    spread = 1 + sum(loads) // (1 << 30)
    return np.cumsum(np.array([max(1, weight // spread) for weight in loads]))


def ranked(own_key, extent, number_of, skew):
    listing = cumulative_ranks(number_of, skew)
    lot = jax.random.randint(jax.random.fold_in(own_key, 1), extent, 0, int(listing[number_of - 1]))
    rank = jnp.searchsorted(jnp.asarray(listing, jnp.int32), lot, side="right")
    return jax.random.permutation(jax.random.fold_in(own_key, 2), number_of)[rank].astype(jnp.int32)


def routed_block(key, own, number, rows, count, top, limit, skew):
    ranking = jax.random.permutation(key, count)
    packed, ordinary = load_shares(count, rows * top, limit, skew, True), load_shares(count, rows * top, limit, skew, False)
    places = jnp.arange(count)

    def named(tallies, turn):
        used = int((tallies > 0).sum())
        fixed = max(1, used // 4)
        moved = fixed + (places - fixed + turn * (used - fixed)) % max(1, count - fixed)
        return jnp.zeros((count,), jnp.int32).at[ranking[jnp.where(places < fixed, places, moved)]].set(jnp.asarray(tallies, jnp.int32))

    tallies = jnp.where(number % 4 == 0, named(packed, number // 4), named(ordinary, number - number // 4 - 1))
    mixed = jax.random.permutation(jax.random.fold_in(own, 3), count)
    source_of, receiver = mixed[0:count // 2 * 2:2], mixed[1:count // 2 * 2:2]
    room = jnp.minimum(tallies[source_of] - 1, limit - tallies[receiver]) // 2
    room = jnp.where((source_of == ranking[0]) | (receiver == ranking[0]) | (tallies[receiver] == 0), 0, jnp.maximum(room, 0))
    moved = jax.random.randint(jax.random.fold_in(own, 4), (count // 2,), 0, 1 << 20) % (room + 1)
    tallies = tallies.at[source_of].add(-moved).at[receiver].add(moved)
    items = jnp.searchsorted(jnp.cumsum(tallies), jnp.arange(rows * top), side="right").astype(jnp.int32)
    grid = items.reshape(top, rows).T
    grid = grid[jax.random.permutation(jax.random.fold_in(own, 1), rows)]
    turn = jax.random.randint(jax.random.fold_in(own, 2), (rows, 1), 0, top)
    return jnp.take_along_axis(grid, (jnp.arange(top)[None, :] + turn) % top, axis=1)


def load_shares(number_of, total, bound, skew, full):
    weights = [(1 << 20) // math.isqrt(rank ** skew) + 1 for rank in range(1, number_of + 1)]
    largest = bound if full else min(bound, max(-(-total // number_of), total * weights[0] // sum(weights)))
    least = 1 if total - largest >= number_of - 1 else 0
    counts, spare = [largest] + [least] * (number_of - 1), total - largest - least * (number_of - 1)
    while spare > 0:
        free = [i for i in range(1, number_of) if counts[i] < largest] or [i for i in range(1, number_of) if counts[i] < bound]
        whole, budget = sum([weights[i] for i in free]), spare
        for i in free:
            addition = min(bound - counts[i], max(1, budget * weights[i] // whole), spare)
            counts[i] = counts[i] + addition
            spare = spare - addition
    return np.array(counts)


def normal_values(key, extent, spread, bound, cuts=(), kind=jnp.bfloat16):
    gain = shard_levels(key, extent, cuts, -0.22, 0.18) if cuts else 1.0
    entries = jax.random.normal(key, extent, jnp.float32) * spread * gain
    return jnp.minimum(jnp.maximum(entries, -bound), bound).astype(kind)


def setup_inputs(seed: int = 0, part: int = 0) -> dict:
    splits = jax.random.split(jax.random.key(seed), 6)
    part_splits = jax.random.split(jax.random.fold_in(splits[5], part), 6)
    tokens = normal_values(part_splits[0], (TOKENS, D), 1.0, 6.0, ((0, 32),))
    expert_ids_keys = jax.random.split(jax.random.fold_in(part_splits[1], 1), TOKENS // TOK_DEV)
    expert_ids_turns = jax.random.permutation(jax.random.fold_in(part_splits[1], 3), TOKENS // TOK_DEV)
    expert_ids = jax.vmap(lambda own, number: routed_block(jax.random.fold_in(part_splits[1], 2), own, number, TOK_DEV, EXPERTS, TOP, MOST, 2))(expert_ids_keys, expert_ids_turns).reshape((TOKENS, TOP))
    gate_logits = normal_values(part_splits[2], (TOKENS, TOP), 1.5, 6.0, ((0, 32),), jnp.float32)
    bin_ids = plant(ranked(part_splits[3], (TOKENS, TOP, BLOCKS), NBINS, 1), jax.random.fold_in(part_splits[3], 3), 0, NBINS - 1).astype(jnp.int32)
    up_weight = normal_values(splits[4], (EXPERTS, D, H), D ** -0.5, 0.09375, ((0, 32),))
    return {"tokens": tokens, "expert_ids": expert_ids, "gate_logits": gate_logits, "bin_ids": bin_ids, "up_weight": up_weight}


route_scale = 2.827


def reference(tokens, expert_ids, gate_logits, bin_ids, up_weight):
    scores = jax.nn.sigmoid(gate_logits.astype(jnp.float32))
    route_weight = (route_scale * scores / jnp.sum(scores, axis=1, keepdims=True)).astype(jnp.bfloat16)
    flat_ids = expert_ids.reshape(-1)
    row_total = flat_ids.shape[0]
    capacity = MOST * N_EXPERT * N_FSDP
    bin_table = bin_ids.reshape(row_total, BLOCKS)
    block_index = jnp.arange(BLOCKS, dtype=jnp.int32)[None, :]

    def one_expert(expert):
        hits = flat_ids == expert
        picked = jnp.nonzero(hits, size=capacity, fill_value=row_total)[0].astype(jnp.int32)
        usable = picked < row_total
        clamped = jnp.where(usable, picked, 0).astype(jnp.int32)
        token_rows = tokens[clamped // TOP]
        up_rows = jnp.dot(token_rows.astype(jnp.float32), up_weight[expert].astype(jnp.float32),
                          precision=lax.Precision.HIGHEST)
        up_rows = jnp.where(usable[:, None], up_rows, jnp.float32(0.0))
        energy = jnp.mean((up_rows * up_rows).reshape(capacity, BLOCKS, BLOCK), axis=2)
        bin_rows = bin_table[clamped]
        histogram = jnp.zeros((BLOCKS, NBINS), jnp.float32).at[block_index, bin_rows].add(energy)
        return up_rows.astype(jnp.bfloat16), picked, histogram

    returned, picked, histogram = lax.map(one_expert, jnp.arange(EXPERTS, dtype=jnp.int32))
    placed = jnp.zeros((row_total + 1, H), jnp.bfloat16).at[picked.reshape(-1)].set(returned.reshape(-1, H))
    up_back = placed[:row_total].reshape(TOKENS, TOP, H)
    mixed = jnp.sum(route_weight.astype(jnp.float32)[:, :, None] * up_back.astype(jnp.float32), axis=1)
    return mixed.astype(jnp.bfloat16), histogram
```

```python
import functools

import jax
import jax.numpy as jnp
from jax import lax
from jax.experimental import pallas as pl
from jax.experimental.pallas import tpu as pltpu
from jax.sharding import PartitionSpec as P

BLOCK = 128
NBINS = 2048
LANES = 128
TILE_N = 256

route_scale = 2.827


def pack_rows(tokens, expert_ids, gate_logits, bin_ids):
    tok_rows, chosen = expert_ids.shape
    scores = jax.nn.sigmoid(gate_logits)
    route_weight = (route_scale * scores / jnp.sum(scores, axis=1, keepdims=True)).astype(
        jnp.bfloat16
    )
    bins = bin_ids.reshape(tok_rows, -1)
    code = ((128 + (bins & 127)) << (bins >> 7)).astype(jnp.float32).astype(jnp.bfloat16)
    tail = jnp.concatenate([expert_ids.astype(jnp.bfloat16), route_weight, code], axis=1)
    tail = jnp.pad(tail, ((0, 0), (0, LANES - tail.shape[1])))
    return jnp.concatenate([tokens, tail], axis=1)


def expert_kernel(chosen, blocks, n_parts, me_ref, *refs):
    parts = refs[:n_parts]
    w_ref = refs[n_parts]
    outs = refs[n_parts + 1 : 2 * n_parts + 1]
    code_ref, energy_ref = refs[2 * n_parts + 1 : 2 * n_parts + 3]
    step = pl.program_id(0)
    width, tile = w_ref.shape

    @pl.when(step == 0)
    def _():
        tail = jnp.concatenate([p[:, width:] for p in parts], axis=0)
        row = lax.broadcasted_iota(jnp.int32, (LANES, LANES), 0)
        col = lax.broadcasted_iota(jnp.int32, (LANES, LANES), 1)
        bins_at = 2 * chosen
        bins_end = bins_at + chosen * blocks
        choice = jnp.where(col < bins_at, col - chosen, (col - bins_at) // blocks)
        carries = (col >= chosen) & (col < bins_end)
        spread = jnp.where((row == choice) & carries, 1.0, 0.0).astype(jnp.bfloat16)
        ids = jnp.dot(tail, spread, preferred_element_type=jnp.float32)
        lane = lax.broadcasted_iota(jnp.int32, tail.shape, 1)
        mine = (
            (ids == me_ref[0].astype(jnp.float32)) & (lane >= chosen) & (lane < bins_end)
        )
        picked = jnp.where(mine, tail, jnp.zeros_like(tail))
        target = jnp.where(row < bins_at, blocks, (row - bins_at) % blocks)
        usable = (row >= chosen) & (row < bins_end)
        fold = jnp.where((col == target) & usable, 1.0, 0.0).astype(jnp.bfloat16)
        code_ref[...] = jnp.dot(picked, fold, preferred_element_type=jnp.float32)
        energy_ref[...] = jnp.zeros_like(energy_ref)

    rows = jnp.concatenate([p[:, :width] for p in parts], axis=0)
    up = jnp.dot(rows, w_ref[...], preferred_element_type=jnp.float32)
    unit = lax.broadcasted_iota(jnp.int32, (tile, LANES), 0)
    lane = lax.broadcasted_iota(jnp.int32, (tile, LANES), 1)
    mean = jnp.where(
        (unit + step * tile) // BLOCK == lane % blocks, 1.0 / BLOCK, 0.0
    ).astype(jnp.bfloat16)
    energy_ref[...] += jnp.dot(
        (up * up).astype(jnp.bfloat16), mean, preferred_element_type=jnp.float32
    )
    weight = code_ref[:, blocks : blocks + 1]
    scaled = (weight * up.astype(jnp.bfloat16).astype(jnp.float32)).astype(jnp.bfloat16)
    at = 0
    for part, out in zip(parts, outs):
        out[...] = scaled[at : at + part.shape[0]]
        at += part.shape[0]


def expert_rows(me, parts, weight, chosen, blocks):
    width, hidden = weight.shape
    total = sum(p.shape[0] for p in parts)
    tile = min(TILE_N, hidden)
    small = jax.ShapeDtypeStruct((total, LANES), jnp.float32)
    return pl.pallas_call(
        functools.partial(expert_kernel, chosen, blocks, len(parts)),
        grid=(hidden // tile,),
        in_specs=[pl.BlockSpec(memory_space=pltpu.SMEM)]
        + [pl.BlockSpec(p.shape, lambda j: (0, 0)) for p in parts]
        + [pl.BlockSpec((width, tile), lambda j: (0, j))],
        out_specs=[pl.BlockSpec((p.shape[0], tile), lambda j: (0, j)) for p in parts]
        + [pl.BlockSpec((total, LANES), lambda j: (0, 0))] * 2,
        out_shape=[jax.ShapeDtypeStruct((p.shape[0], hidden), jnp.bfloat16) for p in parts]
        + [small, small],
        compiler_params=pltpu.CompilerParams(
            dimension_semantics=("arbitrary",), vmem_limit_bytes=24 * 1024 * 1024
        ),
        cost_estimate=pl.CostEstimate(
            flops=2 * total * width * hidden,
            bytes_accessed=2 * width * hidden,
            transcendentals=0,
        ),
        name="expert_rows",
    )(me, *parts, weight)


def histogram_kernel(blocks, n_parts, *refs):
    codes, energies = refs[:n_parts], refs[n_parts : 2 * n_parts]
    out_ref = refs[2 * n_parts]
    levels = NBINS // LANES
    row = lax.broadcasted_iota(jnp.int32, (LANES, LANES), 0)
    col = lax.broadcasted_iota(jnp.int32, (LANES, LANES), 1)
    repeat = jnp.where(row == col % blocks, 1.0, 0.0).astype(jnp.bfloat16)
    wide_row = lax.broadcasted_iota(jnp.int32, (LANES, blocks * LANES), 0)
    wide_col = lax.broadcasted_iota(jnp.int32, (LANES, blocks * LANES), 1)
    stretch = jnp.where(wide_row == wide_col // LANES, 1.0, 0.0).astype(jnp.bfloat16)
    total = jnp.zeros((LANES, blocks * LANES), jnp.float32)
    for code_ref, energy_ref in zip(codes, energies):
        code = code_ref[...]
        lane = lax.broadcasted_iota(jnp.int32, code.shape, 1)
        code = jnp.where(lane < blocks, code, 0.0)
        low = code
        high = jnp.where(code > 0.0, 0.0, -1.0)
        for _ in range(levels - 1):
            above = low >= 256.0
            low = jnp.where(above, low * 0.5, low)
            high = jnp.where(above, high + 1.0, high)
        low = jnp.where(code > 0.0, low - 128.0, -1.0)
        high_all = jnp.dot(high.astype(jnp.bfloat16), repeat, preferred_element_type=jnp.float32)
        low_all = jnp.dot(low.astype(jnp.bfloat16), stretch, preferred_element_type=jnp.float32)
        energy = jnp.where(high_all == (lane // blocks).astype(jnp.float32), energy_ref[...], 0.0)
        near = energy.astype(jnp.bfloat16)
        rest = (energy - near.astype(jnp.float32)).astype(jnp.bfloat16)
        spot = lax.broadcasted_iota(jnp.int32, low_all.shape, 1) % LANES
        onehot = jnp.where(low_all == spot.astype(jnp.float32), 1.0, 0.0).astype(jnp.bfloat16)
        for piece in (near, rest):
            total += lax.dot_general(
                piece, onehot, (((0,), (0,)), ((), ())), preferred_element_type=jnp.float32
            )
    pick = lax.broadcasted_iota(jnp.int32, (blocks, LANES), 0)
    for level in range(levels):
        band = total[level * blocks : (level + 1) * blocks]
        line = jnp.zeros((blocks, LANES), jnp.float32)
        for block in range(blocks):
            line = jnp.where(pick == block, band[:, block * LANES : (block + 1) * LANES], line)
        out_ref[:, level * LANES : (level + 1) * LANES] = line


def expert_histogram(codes, energies, blocks):
    rows = sum(c.shape[0] for c in codes)
    return pl.pallas_call(
        functools.partial(histogram_kernel, blocks, len(codes)),
        out_shape=jax.ShapeDtypeStruct((blocks, NBINS), jnp.float32),
        compiler_params=pltpu.CompilerParams(vmem_limit_bytes=24 * 1024 * 1024),
        cost_estimate=pl.CostEstimate(
            flops=4 * rows * LANES * LANES * blocks,
            bytes_accessed=8 * rows * LANES,
            transcendentals=0,
        ),
        name="expert_histogram",
    )(*codes, *energies)


def swap(array, even, odd=None):
    odd = even if odd is None else odd
    size = lax.axis_size("expert")
    return lax.ppermute(array, "expert", [(i, i ^ (odd if i & 1 else even)) for i in range(size)])


def add32(*arrays):
    return functools.reduce(lambda a, b: a + b, [a.astype(jnp.float32) for a in arrays])


def boxed(packed, me, weight, chosen, blocks):
    layers = [packed, swap(packed, 8), swap(packed, 16), swap(packed, 24)]
    keeps, sends, codes, energies = [], [], [], []
    for rows in layers:
        first = swap(rows, 2, 4)
        second = swap(rows, 4, 2)
        third = swap(first, 4, 2)
        half = jnp.concatenate([rows, first, second, third], axis=0)
        other = swap(half, 1)
        keep, send, code, energy = expert_rows(me, [half, other], weight, chosen, blocks)
        keeps.append(keep)
        sends.append(send)
        codes.append(code)
        energies.append(energy)
    tok_rows = packed.shape[0]
    four = len(layers)
    keep = jnp.stack(keeps).reshape(four, 4, tok_rows, -1)
    came = swap(jnp.stack(sends), 1).reshape(keep.shape)
    partial = add32(keep, came)
    crossed = swap(partial[:, 2:].astype(jnp.bfloat16), 4, 2)
    partial = add32(partial[:, :2], crossed)
    crossed = swap(partial[:, 1].astype(jnp.bfloat16), 2, 4)
    partial = add32(partial[:, 0], crossed)
    home = [swap(partial[i].astype(jnp.bfloat16), 8 * i) for i in range(1, four)]
    mixed = add32(partial[0], *home).astype(jnp.bfloat16)
    return mixed, expert_histogram(codes, energies, blocks)


def plain(packed, me, weight, chosen, blocks):
    rows = lax.all_gather(packed, "expert", axis=0, tiled=True)
    step = LANES if rows.shape[0] % LANES == 0 else packed.shape[0]
    scaled, codes, energies = [], [], []
    for at in range(0, rows.shape[0], step):
        part, code, energy = expert_rows(me, [rows[at : at + step]], weight, chosen, blocks)
        scaled.append(part)
        codes.append(code)
        energies.append(energy)
    mixed = lax.psum_scatter(
        jnp.concatenate(scaled, axis=0).astype(jnp.float32),
        "expert",
        scatter_dimension=0,
        tiled=True,
    )
    return mixed.astype(jnp.bfloat16), expert_histogram(codes, energies, blocks)


def shards(tokens, expert_ids, gate_logits, bin_ids, up_weight):
    chosen, blocks = bin_ids.shape[1:]
    packed = pack_rows(tokens, expert_ids, gate_logits, bin_ids)
    me = lax.axis_index("expert").astype(jnp.int32)[None]
    weight = lax.all_gather(up_weight, "fsdp", axis=1, tiled=True)[0]
    route = boxed if lax.axis_size("expert") == 32 else plain
    mixed, histogram = route(packed, me, weight, chosen, blocks)
    histogram = lax.psum_scatter(histogram[None], "fsdp", scatter_dimension=2, tiled=True)
    return mixed, histogram


def solution(mesh):
    return jax.shard_map(
        shards,
        mesh=mesh,
        in_specs=(
            P(("rep", "expert", "fsdp"), None),
            P(("rep", "expert", "fsdp"), None),
            P(("rep", "expert", "fsdp"), None),
            P(("rep", "expert", "fsdp"), None, None),
            P("expert", "fsdp", None),
        ),
        out_specs=(P(("rep", "expert", "fsdp"), None), P(("rep", "expert"), None, "fsdp")),
        check_vma=False,
    )
```

```python
import functools

import jax
import jax.numpy as jnp
from jax import lax
from jax.experimental import pallas as pl
from jax.experimental.pallas import tpu as pltpu
from jax.sharding import PartitionSpec as P

BLOCK = 128
NBINS = 2048
LANES = 128
TILE_N = 256
K_SLICES = 7

route_scale = 2.827


def pack_kernel(tokens_ref, ids_ref, logits_ref, bins_ref, out_ref):
    tok_rows, width = tokens_ref.shape
    scores = jax.nn.sigmoid(logits_ref[...])
    route_weight = route_scale * scores / jnp.sum(scores, axis=0, keepdims=True)
    bins = bins_ref[...]
    code = ((128 + (bins & 127)) << (bins >> 7)).astype(jnp.float32)
    used = 2 * ids_ref.shape[0] + bins.shape[0]
    tail = jnp.concatenate(
        [
            ids_ref[...].astype(jnp.float32),
            route_weight,
            code,
            jnp.zeros((LANES - used, tok_rows), jnp.float32),
        ],
        axis=0,
    ).astype(jnp.bfloat16)
    row = lax.broadcasted_iota(jnp.int32, (LANES, LANES), 0)
    col = lax.broadcasted_iota(jnp.int32, (LANES, LANES), 1)
    unit = jnp.where(row == col, 1.0, 0.0).astype(jnp.bfloat16)
    turned = lax.dot_general(
        tail, unit, (((0,), (0,)), ((), ())), preferred_element_type=jnp.float32
    )
    out_ref[:, :width] = tokens_ref[...]
    out_ref[:, width:] = turned.astype(jnp.bfloat16)


def pack_rows(tokens, expert_ids, gate_logits, bin_ids):
    tok_rows, width = tokens.shape
    return pl.pallas_call(
        pack_kernel,
        out_shape=jax.ShapeDtypeStruct((tok_rows, width + LANES), jnp.bfloat16),
        name="pack_rows",
    )(
        tokens,
        expert_ids.T,
        gate_logits.T,
        jnp.transpose(bin_ids, (1, 2, 0)).reshape(-1, tok_rows),
    )


def expert_kernel(chosen, blocks, n_parts, me_ref, *refs):
    parts = refs[:n_parts]
    w_ref = refs[n_parts]
    outs = refs[n_parts + 1 : 2 * n_parts + 1]
    code_ref, energy_ref, held, up_ref, sems = refs[2 * n_parts + 1 :]
    width, hidden = w_ref.shape
    tile = min(TILE_N, hidden)
    slices = sems.shape[0]
    depth = width // slices
    copies = [
        pltpu.make_async_copy(
            w_ref.at[pl.ds(i * depth, depth)], held.at[pl.ds(i * depth, depth)], sems.at[i]
        )
        for i in range(slices)
    ]
    for copy in copies:
        copy.start()

    tail = jnp.concatenate([p[:, width:] for p in parts], axis=0)
    row = lax.broadcasted_iota(jnp.int32, (LANES, LANES), 0)
    col = lax.broadcasted_iota(jnp.int32, (LANES, LANES), 1)
    bins_at = 2 * chosen
    bins_end = bins_at + chosen * blocks
    choice = jnp.where(col < bins_at, col - chosen, (col - bins_at) // blocks)
    carries = (col >= chosen) & (col < bins_end)
    spread = jnp.where((row == choice) & carries, 1.0, 0.0).astype(jnp.bfloat16)
    ids = jnp.dot(tail, spread, preferred_element_type=jnp.float32)
    lane = lax.broadcasted_iota(jnp.int32, tail.shape, 1)
    mine = (ids == me_ref[0].astype(jnp.float32)) & (lane >= chosen) & (lane < bins_end)
    picked = jnp.where(mine, tail.astype(jnp.float32), 0.0).astype(jnp.bfloat16)
    target = jnp.where(row < bins_at, blocks, (row - bins_at) % blocks)
    usable = (row >= chosen) & (row < bins_end)
    fold = jnp.where((col == target) & usable, 1.0, 0.0).astype(jnp.bfloat16)
    code = jnp.dot(picked, fold, preferred_element_type=jnp.float32)
    code_ref[...] = code
    weight = code[:, blocks : blocks + 1]

    energy = jnp.zeros(energy_ref.shape, jnp.float32)
    unit = lax.broadcasted_iota(jnp.int32, (tile, LANES), 0)
    slot = lax.broadcasted_iota(jnp.int32, (tile, LANES), 1) % blocks
    for i, copy in enumerate(copies):
        copy.wait()
        span = slice(i * depth, (i + 1) * depth)
        rows = jnp.concatenate([p[:, span] for p in parts], axis=0)
        for j in range(0, hidden, tile):
            term = jnp.dot(rows, held[span, j : j + tile], preferred_element_type=jnp.float32)
            up_ref[:, j : j + tile] = term if i == 0 else up_ref[:, j : j + tile] + term
    for i in range(hidden // tile):
        up = up_ref[:, i * tile : (i + 1) * tile]
        mean = jnp.where((unit + i * tile) // BLOCK == slot, 1.0 / BLOCK, 0.0)
        energy += jnp.dot(
            (up * up).astype(jnp.bfloat16),
            mean.astype(jnp.bfloat16),
            preferred_element_type=jnp.float32,
        )
        scaled = (weight * up.astype(jnp.bfloat16).astype(jnp.float32)).astype(jnp.bfloat16)
        at = 0
        for part, out in zip(parts, outs):
            out[:, i * tile : (i + 1) * tile] = scaled[at : at + part.shape[0]]
            at += part.shape[0]
    energy_ref[...] = energy


def expert_rows(me, parts, weight, chosen, blocks):
    width, hidden = weight.shape
    total = sum(p.shape[0] for p in parts)
    small = jax.ShapeDtypeStruct((total, LANES), jnp.float32)
    inside = pl.BlockSpec(memory_space=pltpu.VMEM)
    return pl.pallas_call(
        functools.partial(expert_kernel, chosen, blocks, len(parts)),
        in_specs=[pl.BlockSpec(memory_space=pltpu.SMEM)]
        + [inside] * len(parts)
        + [pl.BlockSpec(memory_space=pltpu.HBM)],
        out_specs=[inside] * (len(parts) + 2),
        out_shape=[jax.ShapeDtypeStruct((p.shape[0], hidden), jnp.bfloat16) for p in parts]
        + [small, small],
        scratch_shapes=[
            pltpu.VMEM((width, hidden), weight.dtype),
            pltpu.VMEM((total, hidden), jnp.float32),
            pltpu.SemaphoreType.DMA((K_SLICES,)),
        ],
        compiler_params=pltpu.CompilerParams(vmem_limit_bytes=50 * 1024 * 1024),
        cost_estimate=pl.CostEstimate(
            flops=2 * total * width * hidden,
            bytes_accessed=2 * width * hidden,
            transcendentals=0,
        ),
        name="expert_rows",
    )(me, *parts, weight)


def histogram_kernel(blocks, n_parts, *refs):
    codes, energies = refs[:n_parts], refs[n_parts : 2 * n_parts]
    out_ref = refs[2 * n_parts]
    levels = NBINS // LANES
    row = lax.broadcasted_iota(jnp.int32, (LANES, LANES), 0)
    col = lax.broadcasted_iota(jnp.int32, (LANES, LANES), 1)
    repeat = jnp.where(row == col % blocks, 1.0, 0.0).astype(jnp.bfloat16)
    wide_row = lax.broadcasted_iota(jnp.int32, (LANES, blocks * LANES), 0)
    wide_col = lax.broadcasted_iota(jnp.int32, (LANES, blocks * LANES), 1)
    stretch = jnp.where(wide_row == wide_col // LANES, 1.0, 0.0).astype(jnp.bfloat16)
    total = jnp.zeros((LANES, blocks * LANES), jnp.float32)
    for code_ref, energy_ref in zip(codes, energies):
        code = code_ref[...]
        lane = lax.broadcasted_iota(jnp.int32, code.shape, 1)
        code = jnp.where(lane < blocks, code, 0.0)
        low = code
        high = jnp.where(code > 0.0, 0.0, -1.0)
        for _ in range(levels - 1):
            above = low >= 256.0
            low = jnp.where(above, low * 0.5, low)
            high = jnp.where(above, high + 1.0, high)
        low = jnp.where(code > 0.0, low - 128.0, -1.0)
        high_all = jnp.dot(high.astype(jnp.bfloat16), repeat, preferred_element_type=jnp.float32)
        low_all = jnp.dot(low.astype(jnp.bfloat16), stretch, preferred_element_type=jnp.float32)
        energy = jnp.where(high_all == (lane // blocks).astype(jnp.float32), energy_ref[...], 0.0)
        near = energy.astype(jnp.bfloat16)
        rest = (energy - near.astype(jnp.float32)).astype(jnp.bfloat16)
        spot = lax.broadcasted_iota(jnp.int32, low_all.shape, 1) % LANES
        onehot = jnp.where(low_all == spot.astype(jnp.float32), 1.0, 0.0).astype(jnp.bfloat16)
        for piece in (near, rest):
            total += lax.dot_general(
                piece, onehot, (((0,), (0,)), ((), ())), preferred_element_type=jnp.float32
            )
    pick = lax.broadcasted_iota(jnp.int32, (blocks, LANES), 0)
    for level in range(levels):
        band = total[level * blocks : (level + 1) * blocks]
        line = jnp.zeros((blocks, LANES), jnp.float32)
        for block in range(blocks):
            line = jnp.where(pick == block, band[:, block * LANES : (block + 1) * LANES], line)
        out_ref[:, level * LANES : (level + 1) * LANES] = line


def expert_histogram(codes, energies, blocks):
    rows = sum(c.shape[0] for c in codes)
    return pl.pallas_call(
        functools.partial(histogram_kernel, blocks, len(codes)),
        out_shape=jax.ShapeDtypeStruct((blocks, NBINS), jnp.float32),
        compiler_params=pltpu.CompilerParams(vmem_limit_bytes=24 * 1024 * 1024),
        cost_estimate=pl.CostEstimate(
            flops=4 * rows * LANES * LANES * blocks,
            bytes_accessed=8 * rows * LANES,
            transcendentals=0,
        ),
        name="expert_histogram",
    )(*codes, *energies)


def swap(array, even, odd=None):
    odd = even if odd is None else odd
    size = lax.axis_size("expert")
    return lax.ppermute(array, "expert", [(i, i ^ (odd if i & 1 else even)) for i in range(size)])


def add32(*arrays):
    return functools.reduce(lambda a, b: a + b, [a.astype(jnp.float32) for a in arrays])


def boxed(packed, me, weight, chosen, blocks):
    far = swap(packed, 16)
    near = swap(packed, 8)
    layers = [packed, near, far, swap(far, 8)]
    halves, others = [], []
    for rows in [packed, near, jnp.concatenate([far, layers[3]], axis=0)]:
        first = swap(rows, 2, 4)
        second = swap(rows, 4, 2)
        third = swap(first, 4, 2)
        half = jnp.concatenate([rows, first, second, third], axis=0)
        halves.append(half)
        others.append(swap(half, 1))
    four = len(layers)
    *scaled, code, energy = expert_rows(me, halves + others, weight, chosen, blocks)
    tok_rows = packed.shape[0]

    def by_layer(parts):
        near_two = jnp.stack(parts[:2]).reshape(2, 4, tok_rows, -1)
        far_two = jnp.swapaxes(parts[2].reshape(4, 2, tok_rows, -1), 0, 1)
        return jnp.concatenate([near_two, far_two], axis=0)

    keep = by_layer(scaled[:3])
    came = swap(jnp.concatenate(scaled[3:], axis=0), 1)
    came = by_layer([came[: 4 * tok_rows], came[4 * tok_rows : 8 * tok_rows], came[8 * tok_rows :]])
    partial = add32(keep, came)
    crossed = swap(partial[:, 2:].astype(jnp.bfloat16), 4, 2)
    partial = add32(partial[:, :2], crossed)
    crossed = swap(partial[:, 1].astype(jnp.bfloat16), 2, 4)
    partial = add32(partial[:, 0], crossed)
    home = [swap(partial[i].astype(jnp.bfloat16), 8 * i) for i in range(1, four)]
    mixed = add32(partial[0], *home).astype(jnp.bfloat16)
    return mixed, expert_histogram([code], [energy], blocks)


def plain(packed, me, weight, chosen, blocks):
    rows = lax.all_gather(packed, "expert", axis=0, tiled=True)
    step = LANES if rows.shape[0] % LANES == 0 else packed.shape[0]
    scaled, codes, energies = [], [], []
    for at in range(0, rows.shape[0], step):
        part, code, energy = expert_rows(me, [rows[at : at + step]], weight, chosen, blocks)
        scaled.append(part)
        codes.append(code)
        energies.append(energy)
    mixed = lax.psum_scatter(
        jnp.concatenate(scaled, axis=0).astype(jnp.float32),
        "expert",
        scatter_dimension=0,
        tiled=True,
    )
    return mixed.astype(jnp.bfloat16), expert_histogram(codes, energies, blocks)


def shards(tokens, expert_ids, gate_logits, bin_ids, up_weight):
    chosen, blocks = bin_ids.shape[1:]
    packed = pack_rows(tokens, expert_ids, gate_logits, bin_ids)
    me = lax.axis_index("expert").astype(jnp.int32)[None]
    weight = lax.all_gather(up_weight, "fsdp", axis=1, tiled=True)[0]
    route = boxed if lax.axis_size("expert") == 32 else plain
    mixed, histogram = route(packed, me, weight, chosen, blocks)
    histogram = lax.psum_scatter(histogram[None], "fsdp", scatter_dimension=2, tiled=True)
    return mixed, histogram


def solution(mesh):
    return jax.shard_map(
        shards,
        mesh=mesh,
        in_specs=(
            P(("rep", "expert", "fsdp"), None),
            P(("rep", "expert", "fsdp"), None),
            P(("rep", "expert", "fsdp"), None),
            P(("rep", "expert", "fsdp"), None, None),
            P("expert", "fsdp", None),
        ),
        out_specs=(P(("rep", "expert", "fsdp"), None), P(("rep", "expert"), None, "fsdp")),
        check_vma=False,
    )
```

```python
import functools

import jax
import jax.numpy as jnp
from jax import lax
from jax.experimental import pallas as pl
from jax.experimental.pallas import tpu as pltpu
from jax.sharding import PartitionSpec as P

BLOCK = 128
NBINS = 2048
LANES = 128
TILE_N = 256
K_SLICES = 7

route_scale = 2.827


def pack_kernel(tokens_ref, ids_ref, logits_ref, bins_ref, out_ref):
    tok_rows, width = tokens_ref.shape
    scores = jax.nn.sigmoid(logits_ref[...])
    route_weight = route_scale * scores / jnp.sum(scores, axis=0, keepdims=True)
    bins = bins_ref[...]
    code = ((128 + (bins & 127)) << (bins >> 7)).astype(jnp.float32)
    used = 2 * ids_ref.shape[0] + bins.shape[0]
    tail = jnp.concatenate(
        [
            ids_ref[...].astype(jnp.float32),
            route_weight,
            code,
            jnp.zeros((LANES - used, tok_rows), jnp.float32),
        ],
        axis=0,
    ).astype(jnp.bfloat16)
    row = lax.broadcasted_iota(jnp.int32, (LANES, LANES), 0)
    col = lax.broadcasted_iota(jnp.int32, (LANES, LANES), 1)
    unit = jnp.where(row == col, 1.0, 0.0).astype(jnp.bfloat16)
    turned = lax.dot_general(
        tail, unit, (((0,), (0,)), ((), ())), preferred_element_type=jnp.float32
    )
    out_ref[:, :width] = tokens_ref[...]
    out_ref[:, width:] = turned.astype(jnp.bfloat16)


def pack_rows(tokens, expert_ids, gate_logits, bin_ids):
    tok_rows, width = tokens.shape
    return pl.pallas_call(
        pack_kernel,
        out_shape=jax.ShapeDtypeStruct((tok_rows, width + LANES), jnp.bfloat16),
        name="pack_rows",
    )(
        tokens,
        expert_ids.T,
        gate_logits.T,
        jnp.transpose(bin_ids, (1, 2, 0)).reshape(-1, tok_rows),
    )


def expert_kernel(chosen, blocks, n_parts, me_ref, *refs):
    parts = refs[:n_parts]
    w_ref = refs[n_parts]
    outs = refs[n_parts + 1 : 2 * n_parts + 1]
    code_ref, energy_ref, held, up_ref, sems = refs[2 * n_parts + 1 :]
    width, hidden = w_ref.shape
    tile = min(TILE_N, hidden)
    slices = sems.shape[0]
    depth = width // slices
    copies = [
        pltpu.make_async_copy(
            w_ref.at[pl.ds(i * depth, depth)], held.at[pl.ds(i * depth, depth)], sems.at[i]
        )
        for i in range(slices)
    ]
    for copy in copies:
        copy.start()

    tail = jnp.concatenate([p[:, width:] for p in parts], axis=0)
    row = lax.broadcasted_iota(jnp.int32, (LANES, LANES), 0)
    col = lax.broadcasted_iota(jnp.int32, (LANES, LANES), 1)
    bins_at = 2 * chosen
    bins_end = bins_at + chosen * blocks
    choice = jnp.where(col < bins_at, col - chosen, (col - bins_at) // blocks)
    carries = (col >= chosen) & (col < bins_end)
    spread = jnp.where((row == choice) & carries, 1.0, 0.0).astype(jnp.bfloat16)
    ids = jnp.dot(tail, spread, preferred_element_type=jnp.float32)
    lane = lax.broadcasted_iota(jnp.int32, tail.shape, 1)
    mine = (ids == me_ref[0].astype(jnp.float32)) & (lane >= chosen) & (lane < bins_end)
    picked = jnp.where(mine, tail.astype(jnp.float32), 0.0).astype(jnp.bfloat16)
    target = jnp.where(row < bins_at, blocks, (row - bins_at) % blocks)
    usable = (row >= chosen) & (row < bins_end)
    fold = jnp.where((col == target) & usable, 1.0, 0.0).astype(jnp.bfloat16)
    code = jnp.dot(picked, fold, preferred_element_type=jnp.float32)
    code_ref[...] = code
    weight = code[:, blocks : blocks + 1]

    energy = jnp.zeros(energy_ref.shape, jnp.float32)
    unit = lax.broadcasted_iota(jnp.int32, (tile, LANES), 0)
    slot = lax.broadcasted_iota(jnp.int32, (tile, LANES), 1) % blocks
    for i, copy in enumerate(copies):
        copy.wait()
        span = slice(i * depth, (i + 1) * depth)
        rows = jnp.concatenate([p[:, span] for p in parts], axis=0)
        for j in range(0, hidden, tile):
            term = jnp.dot(rows, held[span, j : j + tile], preferred_element_type=jnp.float32)
            up_ref[:, j : j + tile] = term if i == 0 else up_ref[:, j : j + tile] + term
    for i in range(hidden // tile):
        up = up_ref[:, i * tile : (i + 1) * tile]
        mean = jnp.where((unit + i * tile) // BLOCK == slot, 1.0 / BLOCK, 0.0)
        energy += jnp.dot(
            (up * up).astype(jnp.bfloat16),
            mean.astype(jnp.bfloat16),
            preferred_element_type=jnp.float32,
        )
        scaled = (weight * up.astype(jnp.bfloat16).astype(jnp.float32)).astype(jnp.bfloat16)
        at = 0
        for part, out in zip(parts, outs):
            out[:, i * tile : (i + 1) * tile] = scaled[at : at + part.shape[0]]
            at += part.shape[0]
    energy_ref[...] = energy


def expert_rows(me, parts, weight, chosen, blocks):
    width, hidden = weight.shape
    total = sum(p.shape[0] for p in parts)
    small = jax.ShapeDtypeStruct((total, LANES), jnp.float32)
    inside = pl.BlockSpec(memory_space=pltpu.VMEM)
    return pl.pallas_call(
        functools.partial(expert_kernel, chosen, blocks, len(parts)),
        in_specs=[pl.BlockSpec(memory_space=pltpu.SMEM)]
        + [inside] * len(parts)
        + [pl.BlockSpec(memory_space=pltpu.HBM)],
        out_specs=[inside] * (len(parts) + 2),
        out_shape=[jax.ShapeDtypeStruct((p.shape[0], hidden), jnp.bfloat16) for p in parts]
        + [small, small],
        scratch_shapes=[
            pltpu.VMEM((width, hidden), weight.dtype),
            pltpu.VMEM((total, hidden), jnp.float32),
            pltpu.SemaphoreType.DMA((K_SLICES,)),
        ],
        compiler_params=pltpu.CompilerParams(vmem_limit_bytes=50 * 1024 * 1024),
        cost_estimate=pl.CostEstimate(
            flops=2 * total * width * hidden,
            bytes_accessed=2 * width * hidden,
            transcendentals=0,
        ),
        name="expert_rows",
    )(me, *parts, weight)


def histogram_kernel(blocks, n_parts, *refs):
    codes, energies = refs[:n_parts], refs[n_parts : 2 * n_parts]
    out_ref = refs[2 * n_parts]
    levels = NBINS // LANES
    row = lax.broadcasted_iota(jnp.int32, (LANES, LANES), 0)
    col = lax.broadcasted_iota(jnp.int32, (LANES, LANES), 1)
    repeat = jnp.where(row == col % blocks, 1.0, 0.0).astype(jnp.bfloat16)
    wide_row = lax.broadcasted_iota(jnp.int32, (LANES, blocks * LANES), 0)
    wide_col = lax.broadcasted_iota(jnp.int32, (LANES, blocks * LANES), 1)
    stretch = jnp.where(wide_row == wide_col // LANES, 1.0, 0.0).astype(jnp.bfloat16)
    total = jnp.zeros((LANES, blocks * LANES), jnp.float32)
    for code_ref, energy_ref in zip(codes, energies):
        code = code_ref[...]
        lane = lax.broadcasted_iota(jnp.int32, code.shape, 1)
        code = jnp.where(lane < blocks, code, 0.0)
        low = code
        high = jnp.where(code > 0.0, 0.0, -1.0)
        for _ in range(levels - 1):
            above = low >= 256.0
            low = jnp.where(above, low * 0.5, low)
            high = jnp.where(above, high + 1.0, high)
        low = jnp.where(code > 0.0, low - 128.0, -1.0)
        high_all = jnp.dot(high.astype(jnp.bfloat16), repeat, preferred_element_type=jnp.float32)
        low_all = jnp.dot(low.astype(jnp.bfloat16), stretch, preferred_element_type=jnp.float32)
        energy = jnp.where(high_all == (lane // blocks).astype(jnp.float32), energy_ref[...], 0.0)
        near = energy.astype(jnp.bfloat16)
        rest = (energy - near.astype(jnp.float32)).astype(jnp.bfloat16)
        spot = lax.broadcasted_iota(jnp.int32, low_all.shape, 1) % LANES
        onehot = jnp.where(low_all == spot.astype(jnp.float32), 1.0, 0.0).astype(jnp.bfloat16)
        for piece in (near, rest):
            total += lax.dot_general(
                piece, onehot, (((0,), (0,)), ((), ())), preferred_element_type=jnp.float32
            )
    pick = lax.broadcasted_iota(jnp.int32, (blocks, LANES), 0)
    for level in range(levels):
        band = total[level * blocks : (level + 1) * blocks]
        line = jnp.zeros((blocks, LANES), jnp.float32)
        for block in range(blocks):
            line = jnp.where(pick == block, band[:, block * LANES : (block + 1) * LANES], line)
        out_ref[:, level * LANES : (level + 1) * LANES] = line


def expert_histogram(codes, energies, blocks):
    rows = sum(c.shape[0] for c in codes)
    return pl.pallas_call(
        functools.partial(histogram_kernel, blocks, len(codes)),
        out_shape=jax.ShapeDtypeStruct((blocks, NBINS), jnp.float32),
        compiler_params=pltpu.CompilerParams(vmem_limit_bytes=24 * 1024 * 1024),
        cost_estimate=pl.CostEstimate(
            flops=4 * rows * LANES * LANES * blocks,
            bytes_accessed=8 * rows * LANES,
            transcendentals=0,
        ),
        name="expert_histogram",
    )(*codes, *energies)


def swap(array, even, odd=None):
    odd = even if odd is None else odd
    size = lax.axis_size("expert")
    return lax.ppermute(array, "expert", [(i, i ^ (odd if i & 1 else even)) for i in range(size)])


def add32(*arrays):
    return functools.reduce(lambda a, b: a + b, [a.astype(jnp.float32) for a in arrays])


def boxed(packed, me, weight, chosen, blocks):
    far = swap(packed, 16)
    near = swap(packed, 8)
    layers = [packed, near, far, swap(far, 8)]
    halves, others = [], []
    for rows in [packed, near, jnp.concatenate([far, layers[3]], axis=0)]:
        first = swap(rows, 2, 4)
        second = swap(rows, 4, 2)
        third = swap(first, 4, 2)
        half = jnp.concatenate([rows, first, second, third], axis=0)
        halves.append(half)
        others.append(swap(half, 1))
    four = len(layers)
    *scaled, code, energy = expert_rows(me, halves + others, weight, chosen, blocks)
    tok_rows = packed.shape[0]

    def by_layer(parts):
        near_two = jnp.stack(parts[:2]).reshape(2, 4, tok_rows, -1)
        far_two = jnp.swapaxes(parts[2].reshape(4, 2, tok_rows, -1), 0, 1)
        return jnp.concatenate([near_two, far_two], axis=0)

    keep = by_layer(scaled[:3])
    came = swap(jnp.concatenate(scaled[3:], axis=0), 1)
    came = by_layer([came[: 4 * tok_rows], came[4 * tok_rows : 8 * tok_rows], came[8 * tok_rows :]])
    partial = add32(keep, came)
    leaving = partial[:, 1:].astype(jnp.bfloat16)
    partial = add32(
        partial[:, 0],
        swap(leaving[:, 2], 6),
        swap(leaving[:, 0], 2, 4),
        swap(leaving[:, 1], 4, 2),
    )
    home = [swap(partial[i].astype(jnp.bfloat16), 8 * i) for i in range(1, four)]
    mixed = add32(partial[0], *home).astype(jnp.bfloat16)
    return mixed, expert_histogram([code], [energy], blocks)


def plain(packed, me, weight, chosen, blocks):
    rows = lax.all_gather(packed, "expert", axis=0, tiled=True)
    step = LANES if rows.shape[0] % LANES == 0 else packed.shape[0]
    scaled, codes, energies = [], [], []
    for at in range(0, rows.shape[0], step):
        part, code, energy = expert_rows(me, [rows[at : at + step]], weight, chosen, blocks)
        scaled.append(part)
        codes.append(code)
        energies.append(energy)
    mixed = lax.psum_scatter(
        jnp.concatenate(scaled, axis=0).astype(jnp.float32),
        "expert",
        scatter_dimension=0,
        tiled=True,
    )
    return mixed.astype(jnp.bfloat16), expert_histogram(codes, energies, blocks)


def shards(tokens, expert_ids, gate_logits, bin_ids, up_weight):
    chosen, blocks = bin_ids.shape[1:]
    packed = pack_rows(tokens, expert_ids, gate_logits, bin_ids)
    me = lax.axis_index("expert").astype(jnp.int32)[None]
    weight = lax.all_gather(up_weight, "fsdp", axis=1, tiled=True)[0]
    route = boxed if lax.axis_size("expert") == 32 else plain
    mixed, histogram = route(packed, me, weight, chosen, blocks)
    histogram = lax.psum_scatter(histogram[None], "fsdp", scatter_dimension=2, tiled=True)
    return mixed, histogram


def solution(mesh):
    return jax.shard_map(
        shards,
        mesh=mesh,
        in_specs=(
            P(("rep", "expert", "fsdp"), None),
            P(("rep", "expert", "fsdp"), None),
            P(("rep", "expert", "fsdp"), None),
            P(("rep", "expert", "fsdp"), None, None),
            P("expert", "fsdp", None),
        ),
        out_specs=(P(("rep", "expert", "fsdp"), None), P(("rep", "expert"), None, "fsdp")),
        check_vma=False,
    )
```

```python
import functools

import jax
import jax.numpy as jnp
from jax import lax
from jax.experimental import pallas as pl
from jax.experimental.pallas import tpu as pltpu
from jax.sharding import PartitionSpec as P

BLOCK = 128
NBINS = 2048
LANES = 128
TILE_N = 256
K_SLICES = 7

route_scale = 2.827


def pack_kernel(tokens_ref, ids_ref, logits_ref, bins_ref, out_ref):
    tok_rows, width = tokens_ref.shape
    scores = jax.nn.sigmoid(logits_ref[...])
    route_weight = route_scale * scores / jnp.sum(scores, axis=0, keepdims=True)
    bins = bins_ref[...]
    code = ((128 + (bins & 127)) << (bins >> 7)).astype(jnp.float32)
    used = 2 * ids_ref.shape[0] + bins.shape[0]
    tail = jnp.concatenate(
        [
            ids_ref[...].astype(jnp.float32),
            route_weight,
            code,
            jnp.zeros((LANES - used, tok_rows), jnp.float32),
        ],
        axis=0,
    ).astype(jnp.bfloat16)
    row = lax.broadcasted_iota(jnp.int32, (LANES, LANES), 0)
    col = lax.broadcasted_iota(jnp.int32, (LANES, LANES), 1)
    unit = jnp.where(row == col, 1.0, 0.0).astype(jnp.bfloat16)
    turned = lax.dot_general(
        tail, unit, (((0,), (0,)), ((), ())), preferred_element_type=jnp.float32
    )
    out_ref[:, :width] = tokens_ref[...]
    out_ref[:, width:] = turned.astype(jnp.bfloat16)


def pack_rows(tokens, expert_ids, gate_logits, bin_ids):
    tok_rows, width = tokens.shape
    return pl.pallas_call(
        pack_kernel,
        out_shape=jax.ShapeDtypeStruct((tok_rows, width + LANES), jnp.bfloat16),
        name="pack_rows",
    )(
        tokens,
        expert_ids.T,
        gate_logits.T,
        jnp.transpose(bin_ids, (1, 2, 0)).reshape(-1, tok_rows),
    )


def expert_kernel(chosen, blocks, n_parts, me_ref, *refs):
    parts = refs[:n_parts]
    w_ref = refs[n_parts]
    outs = refs[n_parts + 1 : 2 * n_parts + 1]
    code_ref, energy_ref, held, up_ref, sems = refs[2 * n_parts + 1 :]
    width, hidden = w_ref.shape
    tile = min(TILE_N, hidden)
    slices = sems.shape[0]
    depth = width // slices
    copies = [
        pltpu.make_async_copy(
            w_ref.at[pl.ds(i * depth, depth)], held.at[pl.ds(i * depth, depth)], sems.at[i]
        )
        for i in range(slices)
    ]
    for copy in copies:
        copy.start()

    tail = jnp.concatenate([p[:, width:] for p in parts], axis=0)
    row = lax.broadcasted_iota(jnp.int32, (LANES, LANES), 0)
    col = lax.broadcasted_iota(jnp.int32, (LANES, LANES), 1)
    bins_at = 2 * chosen
    bins_end = bins_at + chosen * blocks
    choice = jnp.where(col < bins_at, col - chosen, (col - bins_at) // blocks)
    carries = (col >= chosen) & (col < bins_end)
    spread = jnp.where((row == choice) & carries, 1.0, 0.0).astype(jnp.bfloat16)
    ids = jnp.dot(tail, spread, preferred_element_type=jnp.float32)
    lane = lax.broadcasted_iota(jnp.int32, tail.shape, 1)
    mine = (ids == me_ref[0].astype(jnp.float32)) & (lane >= chosen) & (lane < bins_end)
    picked = jnp.where(mine, tail.astype(jnp.float32), 0.0).astype(jnp.bfloat16)
    target = jnp.where(row < bins_at, blocks, (row - bins_at) % blocks)
    usable = (row >= chosen) & (row < bins_end)
    fold = jnp.where((col == target) & usable, 1.0, 0.0).astype(jnp.bfloat16)
    code = jnp.dot(picked, fold, preferred_element_type=jnp.float32)
    code_ref[...] = code
    weight = code[:, blocks : blocks + 1]

    energy = jnp.zeros(energy_ref.shape, jnp.float32)
    unit = lax.broadcasted_iota(jnp.int32, (tile, LANES), 0)
    slot = lax.broadcasted_iota(jnp.int32, (tile, LANES), 1) % blocks
    for i, copy in enumerate(copies):
        copy.wait()
        span = slice(i * depth, (i + 1) * depth)
        rows = jnp.concatenate([p[:, span] for p in parts], axis=0)
        for j in range(0, hidden, tile):
            term = jnp.dot(rows, held[span, j : j + tile], preferred_element_type=jnp.float32)
            up_ref[:, j : j + tile] = term if i == 0 else up_ref[:, j : j + tile] + term
    for i in range(hidden // tile):
        up = up_ref[:, i * tile : (i + 1) * tile]
        mean = jnp.where((unit + i * tile) // BLOCK == slot, 1.0 / BLOCK, 0.0)
        energy += jnp.dot(
            (up * up).astype(jnp.bfloat16),
            mean.astype(jnp.bfloat16),
            preferred_element_type=jnp.float32,
        )
        scaled = (weight * up.astype(jnp.bfloat16).astype(jnp.float32)).astype(jnp.bfloat16)
        at = 0
        for part, out in zip(parts, outs):
            out[:, i * tile : (i + 1) * tile] = scaled[at : at + part.shape[0]]
            at += part.shape[0]
    energy_ref[...] = energy


def expert_rows(me, parts, weight, chosen, blocks):
    width, hidden = weight.shape
    total = sum(p.shape[0] for p in parts)
    small = jax.ShapeDtypeStruct((total, LANES), jnp.float32)
    inside = pl.BlockSpec(memory_space=pltpu.VMEM)
    return pl.pallas_call(
        functools.partial(expert_kernel, chosen, blocks, len(parts)),
        in_specs=[pl.BlockSpec(memory_space=pltpu.SMEM)]
        + [inside] * len(parts)
        + [pl.BlockSpec(memory_space=pltpu.HBM)],
        out_specs=[inside] * (len(parts) + 2),
        out_shape=[jax.ShapeDtypeStruct((p.shape[0], hidden), jnp.bfloat16) for p in parts]
        + [small, small],
        scratch_shapes=[
            pltpu.VMEM((width, hidden), weight.dtype),
            pltpu.VMEM((total, hidden), jnp.float32),
            pltpu.SemaphoreType.DMA((K_SLICES,)),
        ],
        compiler_params=pltpu.CompilerParams(vmem_limit_bytes=50 * 1024 * 1024),
        cost_estimate=pl.CostEstimate(
            flops=2 * total * width * hidden,
            bytes_accessed=2 * width * hidden,
            transcendentals=0,
        ),
        name="expert_rows",
    )(me, *parts, weight)


def histogram_kernel(blocks, n_parts, *refs):
    codes, energies = refs[:n_parts], refs[n_parts : 2 * n_parts]
    out_ref = refs[2 * n_parts]
    levels = NBINS // LANES
    row = lax.broadcasted_iota(jnp.int32, (LANES, LANES), 0)
    col = lax.broadcasted_iota(jnp.int32, (LANES, LANES), 1)
    repeat = jnp.where(row == col % blocks, 1.0, 0.0).astype(jnp.bfloat16)
    wide_row = lax.broadcasted_iota(jnp.int32, (LANES, blocks * LANES), 0)
    wide_col = lax.broadcasted_iota(jnp.int32, (LANES, blocks * LANES), 1)
    stretch = jnp.where(wide_row == wide_col // LANES, 1.0, 0.0).astype(jnp.bfloat16)
    total = jnp.zeros((LANES, blocks * LANES), jnp.float32)
    for code_ref, energy_ref in zip(codes, energies):
        code = code_ref[...]
        lane = lax.broadcasted_iota(jnp.int32, code.shape, 1)
        code = jnp.where(lane < blocks, code, 0.0)
        low = code
        high = jnp.where(code > 0.0, 0.0, -1.0)
        for _ in range(levels - 1):
            above = low >= 256.0
            low = jnp.where(above, low * 0.5, low)
            high = jnp.where(above, high + 1.0, high)
        low = jnp.where(code > 0.0, low - 128.0, -1.0)
        high_all = jnp.dot(high.astype(jnp.bfloat16), repeat, preferred_element_type=jnp.float32)
        low_all = jnp.dot(low.astype(jnp.bfloat16), stretch, preferred_element_type=jnp.float32)
        energy = jnp.where(high_all == (lane // blocks).astype(jnp.float32), energy_ref[...], 0.0)
        near = energy.astype(jnp.bfloat16)
        rest = (energy - near.astype(jnp.float32)).astype(jnp.bfloat16)
        spot = lax.broadcasted_iota(jnp.int32, low_all.shape, 1) % LANES
        onehot = jnp.where(low_all == spot.astype(jnp.float32), 1.0, 0.0).astype(jnp.bfloat16)
        for piece in (near, rest):
            total += lax.dot_general(
                piece, onehot, (((0,), (0,)), ((), ())), preferred_element_type=jnp.float32
            )
    pick = lax.broadcasted_iota(jnp.int32, (blocks, LANES), 0)
    for level in range(levels):
        band = total[level * blocks : (level + 1) * blocks]
        line = jnp.zeros((blocks, LANES), jnp.float32)
        for block in range(blocks):
            line = jnp.where(pick == block, band[:, block * LANES : (block + 1) * LANES], line)
        out_ref[:, level * LANES : (level + 1) * LANES] = line


def expert_histogram(codes, energies, blocks):
    rows = sum(c.shape[0] for c in codes)
    return pl.pallas_call(
        functools.partial(histogram_kernel, blocks, len(codes)),
        out_shape=jax.ShapeDtypeStruct((blocks, NBINS), jnp.float32),
        compiler_params=pltpu.CompilerParams(vmem_limit_bytes=24 * 1024 * 1024),
        cost_estimate=pl.CostEstimate(
            flops=4 * rows * LANES * LANES * blocks,
            bytes_accessed=8 * rows * LANES,
            transcendentals=0,
        ),
        name="expert_histogram",
    )(*codes, *energies)


def swap(array, even, odd=None):
    odd = even if odd is None else odd
    size = lax.axis_size("expert")
    return lax.ppermute(array, "expert", [(i, i ^ (odd if i & 1 else even)) for i in range(size)])


def add32(*arrays):
    return functools.reduce(lambda a, b: a + b, [a.astype(jnp.float32) for a in arrays])


def after(array, *others):
    return lax.optimization_barrier((array, *others))[0]


def boxed(packed, me, weight, chosen, blocks):
    far = swap(packed, 16)
    near = swap(packed, 8)
    layers = [packed, near, far, swap(far, 8)]
    halves, others = [], []
    for rows in [packed, near]:
        first = swap(rows, 2, 4)
        second = swap(rows, 4, 2)
        third = swap(first, 4, 2)
        half = jnp.concatenate([rows, first, second, third], axis=0)
        halves.append(half)
        others.append(swap(half, 1))
    fars = jnp.concatenate([far, layers[3]], axis=0)
    first = swap(fars, 2, 4)
    second = swap(fars, 4, 2)
    early = jnp.concatenate([fars, first, second], axis=0)
    early = after(early, others[0])
    early_other = swap(early, 1)
    third = swap(first, 4, 2)
    third_other = swap(third, 1)
    four = len(layers)
    *scaled, code, energy = expert_rows(
        me, halves + [early, third] + others + [early_other, third_other], weight, chosen, blocks
    )
    scaled = [
        *scaled[:2],
        jnp.concatenate(scaled[2:4], axis=0),
        *scaled[4:6],
        jnp.concatenate(scaled[6:8], axis=0),
    ]
    tok_rows = packed.shape[0]

    def by_layer(parts):
        near_two = jnp.stack(parts[:2]).reshape(2, 4, tok_rows, -1)
        far_two = jnp.swapaxes(parts[2].reshape(4, 2, tok_rows, -1), 0, 1)
        return jnp.concatenate([near_two, far_two], axis=0)

    keep = by_layer(scaled[:3])
    came = swap(jnp.concatenate(scaled[3:], axis=0), 1)
    came = by_layer([came[: 4 * tok_rows], came[4 * tok_rows : 8 * tok_rows], came[8 * tok_rows :]])
    partial = add32(keep, came)
    leaving = partial[:, 1:].astype(jnp.bfloat16)
    partial = add32(
        partial[:, 0],
        swap(leaving[:, 2], 6),
        swap(leaving[:, 0], 2, 4),
        swap(leaving[:, 1], 4, 2),
    )
    home = [swap(partial[i].astype(jnp.bfloat16), 8 * i) for i in range(1, four)]
    mixed = add32(partial[0], *home).astype(jnp.bfloat16)
    return mixed, expert_histogram([code], [energy], blocks)


def plain(packed, me, weight, chosen, blocks):
    rows = lax.all_gather(packed, "expert", axis=0, tiled=True)
    step = LANES if rows.shape[0] % LANES == 0 else packed.shape[0]
    scaled, codes, energies = [], [], []
    for at in range(0, rows.shape[0], step):
        part, code, energy = expert_rows(me, [rows[at : at + step]], weight, chosen, blocks)
        scaled.append(part)
        codes.append(code)
        energies.append(energy)
    mixed = lax.psum_scatter(
        jnp.concatenate(scaled, axis=0).astype(jnp.float32),
        "expert",
        scatter_dimension=0,
        tiled=True,
    )
    return mixed.astype(jnp.bfloat16), expert_histogram(codes, energies, blocks)


def shards(tokens, expert_ids, gate_logits, bin_ids, up_weight):
    chosen, blocks = bin_ids.shape[1:]
    packed = pack_rows(tokens, expert_ids, gate_logits, bin_ids)
    me = lax.axis_index("expert").astype(jnp.int32)[None]
    weight = lax.all_gather(up_weight, "fsdp", axis=1, tiled=True)[0]
    route = boxed if lax.axis_size("expert") == 32 else plain
    mixed, histogram = route(packed, me, weight, chosen, blocks)
    histogram = lax.psum_scatter(histogram[None], "fsdp", scatter_dimension=2, tiled=True)
    return mixed, histogram


def solution(mesh):
    return jax.shard_map(
        shards,
        mesh=mesh,
        in_specs=(
            P(("rep", "expert", "fsdp"), None),
            P(("rep", "expert", "fsdp"), None),
            P(("rep", "expert", "fsdp"), None),
            P(("rep", "expert", "fsdp"), None, None),
            P("expert", "fsdp", None),
        ),
        out_specs=(P(("rep", "expert", "fsdp"), None), P(("rep", "expert"), None, "fsdp")),
        check_vma=False,
    )
```

```python
import functools

import jax
import jax.numpy as jnp
from jax import lax
from jax.experimental import pallas as pl
from jax.experimental.pallas import tpu as pltpu
from jax.sharding import PartitionSpec as P

BLOCK = 128
NBINS = 2048
LANES = 128
TILE_N = 256

route_scale = 2.827


def pack_kernel(tokens_ref, ids_ref, logits_ref, bins_ref, out_ref):
    tok_rows, width = tokens_ref.shape
    scores = jax.nn.sigmoid(logits_ref[...])
    route_weight = route_scale * scores / jnp.sum(scores, axis=0, keepdims=True)
    bins = bins_ref[...]
    code = ((128 + (bins & 127)) << (bins >> 7)).astype(jnp.float32)
    used = 2 * ids_ref.shape[0] + bins.shape[0]
    tail = jnp.concatenate(
        [
            ids_ref[...].astype(jnp.float32),
            route_weight,
            code,
            jnp.zeros((LANES - used, tok_rows), jnp.float32),
        ],
        axis=0,
    ).astype(jnp.bfloat16)
    row = lax.broadcasted_iota(jnp.int32, (LANES, LANES), 0)
    col = lax.broadcasted_iota(jnp.int32, (LANES, LANES), 1)
    unit = jnp.where(row == col, 1.0, 0.0).astype(jnp.bfloat16)
    turned = lax.dot_general(
        tail, unit, (((0,), (0,)), ((), ())), preferred_element_type=jnp.float32
    )
    out_ref[:, :width] = tokens_ref[...]
    out_ref[:, width:] = turned.astype(jnp.bfloat16)


def pack_rows(tokens, expert_ids, gate_logits, bin_ids):
    tok_rows, width = tokens.shape
    return pl.pallas_call(
        pack_kernel,
        out_shape=jax.ShapeDtypeStruct((tok_rows, width + LANES), jnp.bfloat16),
        name="pack_rows",
    )(
        tokens,
        expert_ids.T,
        gate_logits.T,
        jnp.transpose(bin_ids, (1, 2, 0)).reshape(-1, tok_rows),
    )


def weight_spans(width):
    unit = width // 14
    depths = [unit * n for n in (1, 2, 3, 4)]
    depths.append(width - sum(depths))
    return [(sum(depths[:i]), depth) for i, depth in enumerate(depths)]


def expert_kernel(chosen, blocks, n_parts, me_ref, *refs):
    parts = refs[:n_parts]
    w_ref = refs[n_parts]
    outs = refs[n_parts + 1 : 2 * n_parts + 1]
    code_ref, energy_ref, held, up_ref, sems = refs[2 * n_parts + 1 :]
    width, hidden = w_ref.shape
    tile = min(TILE_N, hidden)
    slices = sems.shape[0]
    spans = weight_spans(width)
    copies = [
        pltpu.make_async_copy(
            w_ref.at[pl.ds(start, depth)], held.at[pl.ds(start, depth)], sems.at[i]
        )
        for i, (start, depth) in enumerate(spans)
    ]
    for copy in copies:
        copy.start()

    tail = jnp.concatenate([p[:, width:] for p in parts], axis=0)
    row = lax.broadcasted_iota(jnp.int32, (LANES, LANES), 0)
    col = lax.broadcasted_iota(jnp.int32, (LANES, LANES), 1)
    bins_at = 2 * chosen
    bins_end = bins_at + chosen * blocks
    choice = jnp.where(col < bins_at, col - chosen, (col - bins_at) // blocks)
    carries = (col >= chosen) & (col < bins_end)
    spread = jnp.where((row == choice) & carries, 1.0, 0.0).astype(jnp.bfloat16)
    ids = jnp.dot(tail, spread, preferred_element_type=jnp.float32)
    lane = lax.broadcasted_iota(jnp.int32, tail.shape, 1)
    mine = (ids == me_ref[0].astype(jnp.float32)) & (lane >= chosen) & (lane < bins_end)
    picked = jnp.where(mine, tail.astype(jnp.float32), 0.0).astype(jnp.bfloat16)
    target = jnp.where(row < bins_at, blocks, (row - bins_at) % blocks)
    usable = (row >= chosen) & (row < bins_end)
    fold = jnp.where((col == target) & usable, 1.0, 0.0).astype(jnp.bfloat16)
    code = jnp.dot(picked, fold, preferred_element_type=jnp.float32)
    code_ref[...] = code
    weight = code[:, blocks : blocks + 1]

    energy = jnp.zeros(energy_ref.shape, jnp.float32)
    unit = lax.broadcasted_iota(jnp.int32, (tile, LANES), 0)
    slot = lax.broadcasted_iota(jnp.int32, (tile, LANES), 1) % blocks
    for i, copy in enumerate(copies):
        copy.wait()
        span = slice(spans[i][0], sum(spans[i]))
        rows = jnp.concatenate([p[:, span] for p in parts], axis=0)
        for j in range(0, hidden, tile):
            up = jnp.dot(rows, held[span, j : j + tile], preferred_element_type=jnp.float32)
            if i > 0:
                up += up_ref[:, j : j + tile]
            if i < slices - 1:
                up_ref[:, j : j + tile] = up
                continue
            mean = jnp.where((unit + j) // BLOCK == slot, 1.0 / BLOCK, 0.0)
            energy += jnp.dot(
                (up * up).astype(jnp.bfloat16),
                mean.astype(jnp.bfloat16),
                preferred_element_type=jnp.float32,
            )
            scaled = (weight * up.astype(jnp.bfloat16).astype(jnp.float32)).astype(jnp.bfloat16)
            at = 0
            for part, out in zip(parts, outs):
                out[:, j : j + tile] = scaled[at : at + part.shape[0]]
                at += part.shape[0]
    energy_ref[...] = energy


def expert_rows(me, parts, weight, chosen, blocks):
    width, hidden = weight.shape
    total = sum(p.shape[0] for p in parts)
    small = jax.ShapeDtypeStruct((total, LANES), jnp.float32)
    inside = pl.BlockSpec(memory_space=pltpu.VMEM)
    return pl.pallas_call(
        functools.partial(expert_kernel, chosen, blocks, len(parts)),
        in_specs=[pl.BlockSpec(memory_space=pltpu.SMEM)]
        + [inside] * len(parts)
        + [pl.BlockSpec(memory_space=pltpu.HBM)],
        out_specs=[inside] * (len(parts) + 2),
        out_shape=[jax.ShapeDtypeStruct((p.shape[0], hidden), jnp.bfloat16) for p in parts]
        + [small, small],
        scratch_shapes=[
            pltpu.VMEM((width, hidden), weight.dtype),
            pltpu.VMEM((total, hidden), jnp.float32),
            pltpu.SemaphoreType.DMA((len(weight_spans(width)),)),
        ],
        compiler_params=pltpu.CompilerParams(vmem_limit_bytes=50 * 1024 * 1024),
        cost_estimate=pl.CostEstimate(
            flops=2 * total * width * hidden,
            bytes_accessed=2 * width * hidden,
            transcendentals=0,
        ),
        name="expert_rows",
    )(me, *parts, weight)


def histogram_kernel(blocks, n_parts, *refs):
    codes, energies = refs[:n_parts], refs[n_parts : 2 * n_parts]
    out_ref = refs[2 * n_parts]
    levels = NBINS // LANES
    row = lax.broadcasted_iota(jnp.int32, (LANES, LANES), 0)
    col = lax.broadcasted_iota(jnp.int32, (LANES, LANES), 1)
    repeat = jnp.where(row == col % blocks, 1.0, 0.0).astype(jnp.bfloat16)
    wide_row = lax.broadcasted_iota(jnp.int32, (LANES, blocks * LANES), 0)
    wide_col = lax.broadcasted_iota(jnp.int32, (LANES, blocks * LANES), 1)
    stretch = jnp.where(wide_row == wide_col // LANES, 1.0, 0.0).astype(jnp.bfloat16)
    total = jnp.zeros((LANES, blocks * LANES), jnp.float32)
    for code_ref, energy_ref in zip(codes, energies):
        code = code_ref[...]
        lane = lax.broadcasted_iota(jnp.int32, code.shape, 1)
        code = jnp.where(lane < blocks, code, 0.0)
        low = code
        high = jnp.where(code > 0.0, 0.0, -1.0)
        for _ in range(levels - 1):
            above = low >= 256.0
            low = jnp.where(above, low * 0.5, low)
            high = jnp.where(above, high + 1.0, high)
        low = jnp.where(code > 0.0, low - 128.0, -1.0)
        high_all = jnp.dot(high.astype(jnp.bfloat16), repeat, preferred_element_type=jnp.float32)
        low_all = jnp.dot(low.astype(jnp.bfloat16), stretch, preferred_element_type=jnp.float32)
        energy = jnp.where(high_all == (lane // blocks).astype(jnp.float32), energy_ref[...], 0.0)
        near = energy.astype(jnp.bfloat16)
        rest = (energy - near.astype(jnp.float32)).astype(jnp.bfloat16)
        spot = lax.broadcasted_iota(jnp.int32, low_all.shape, 1) % LANES
        onehot = jnp.where(low_all == spot.astype(jnp.float32), 1.0, 0.0).astype(jnp.bfloat16)
        for piece in (near, rest):
            total += lax.dot_general(
                piece, onehot, (((0,), (0,)), ((), ())), preferred_element_type=jnp.float32
            )
    pick = lax.broadcasted_iota(jnp.int32, (blocks, LANES), 0)
    for level in range(levels):
        band = total[level * blocks : (level + 1) * blocks]
        line = jnp.zeros((blocks, LANES), jnp.float32)
        for block in range(blocks):
            line = jnp.where(pick == block, band[:, block * LANES : (block + 1) * LANES], line)
        out_ref[:, level * LANES : (level + 1) * LANES] = line


def expert_histogram(codes, energies, blocks):
    rows = sum(c.shape[0] for c in codes)
    return pl.pallas_call(
        functools.partial(histogram_kernel, blocks, len(codes)),
        out_shape=jax.ShapeDtypeStruct((blocks, NBINS), jnp.float32),
        compiler_params=pltpu.CompilerParams(vmem_limit_bytes=24 * 1024 * 1024),
        cost_estimate=pl.CostEstimate(
            flops=4 * rows * LANES * LANES * blocks,
            bytes_accessed=8 * rows * LANES,
            transcendentals=0,
        ),
        name="expert_histogram",
    )(*codes, *energies)


def swap(array, even, odd=None):
    odd = even if odd is None else odd
    size = lax.axis_size("expert")
    return lax.ppermute(array, "expert", [(i, i ^ (odd if i & 1 else even)) for i in range(size)])


def add32(*arrays):
    return functools.reduce(lambda a, b: a + b, [a.astype(jnp.float32) for a in arrays])


def after(array, *others):
    return lax.optimization_barrier((array, *others))[0]


def boxed(packed, me, weight, chosen, blocks):
    far = swap(packed, 16)
    near = swap(packed, 8)
    layers = [packed, near, far, swap(far, 8)]
    halves, others = [], []
    for rows in [packed, near]:
        first = swap(rows, 2, 4)
        second = swap(rows, 4, 2)
        third = swap(first, 4, 2)
        half = jnp.concatenate([rows, first, second, third], axis=0)
        halves.append(half)
        others.append(swap(half, 1))
    fars = jnp.concatenate([far, layers[3]], axis=0)
    first = swap(fars, 2, 4)
    second = swap(fars, 4, 2)
    early = jnp.concatenate([fars, first, second], axis=0)
    early = after(early, others[0])
    early_other = swap(early, 1)
    third = swap(first, 4, 2)
    third_other = swap(third, 1)
    four = len(layers)
    *scaled, code, energy = expert_rows(
        me, halves + [early, third] + others + [early_other, third_other], weight, chosen, blocks
    )
    scaled = [
        *scaled[:2],
        jnp.concatenate(scaled[2:4], axis=0),
        *scaled[4:6],
        jnp.concatenate(scaled[6:8], axis=0),
    ]
    tok_rows = packed.shape[0]

    def by_layer(parts):
        near_two = jnp.stack(parts[:2]).reshape(2, 4, tok_rows, -1)
        far_two = jnp.swapaxes(parts[2].reshape(4, 2, tok_rows, -1), 0, 1)
        return jnp.concatenate([near_two, far_two], axis=0)

    keep = by_layer(scaled[:3])
    came = swap(jnp.concatenate(scaled[3:], axis=0), 1)
    came = by_layer([came[: 4 * tok_rows], came[4 * tok_rows : 8 * tok_rows], came[8 * tok_rows :]])
    partial = add32(keep, came)
    leaving = partial[:, 1:].astype(jnp.bfloat16)
    partial = add32(
        partial[:, 0],
        swap(leaving[:, 2], 6),
        swap(leaving[:, 0], 2, 4),
        swap(leaving[:, 1], 4, 2),
    )
    histogram = expert_histogram([code], [energy], blocks)
    partial = after(partial, histogram)
    home = [swap(partial[i].astype(jnp.bfloat16), 8 * i) for i in range(1, four)]
    mixed = add32(partial[0], *home).astype(jnp.bfloat16)
    return mixed, histogram


def plain(packed, me, weight, chosen, blocks):
    rows = lax.all_gather(packed, "expert", axis=0, tiled=True)
    step = LANES if rows.shape[0] % LANES == 0 else packed.shape[0]
    scaled, codes, energies = [], [], []
    for at in range(0, rows.shape[0], step):
        part, code, energy = expert_rows(me, [rows[at : at + step]], weight, chosen, blocks)
        scaled.append(part)
        codes.append(code)
        energies.append(energy)
    mixed = lax.psum_scatter(
        jnp.concatenate(scaled, axis=0).astype(jnp.float32),
        "expert",
        scatter_dimension=0,
        tiled=True,
    )
    return mixed.astype(jnp.bfloat16), expert_histogram(codes, energies, blocks)


def shards(tokens, expert_ids, gate_logits, bin_ids, up_weight):
    chosen, blocks = bin_ids.shape[1:]
    packed = pack_rows(tokens, expert_ids, gate_logits, bin_ids)
    me = lax.axis_index("expert").astype(jnp.int32)[None]
    weight = lax.all_gather(up_weight, "fsdp", axis=1, tiled=True)[0]
    route = boxed if lax.axis_size("expert") == 32 else plain
    mixed, histogram = route(packed, me, weight, chosen, blocks)
    histogram = lax.psum_scatter(histogram[None], "fsdp", scatter_dimension=2, tiled=True)
    return mixed, histogram


def solution(mesh):
    return jax.shard_map(
        shards,
        mesh=mesh,
        in_specs=(
            P(("rep", "expert", "fsdp"), None),
            P(("rep", "expert", "fsdp"), None),
            P(("rep", "expert", "fsdp"), None),
            P(("rep", "expert", "fsdp"), None, None),
            P("expert", "fsdp", None),
        ),
        out_specs=(P(("rep", "expert", "fsdp"), None), P(("rep", "expert"), None, "fsdp")),
        check_vma=False,
    )
```

```python
import functools

import jax
import jax.numpy as jnp
from jax import lax
from jax.experimental import pallas as pl
from jax.experimental.pallas import tpu as pltpu
from jax.sharding import PartitionSpec as P

BLOCK = 128
NBINS = 2048
LANES = 128
TILE_N = 256

route_scale = 2.827


def pack_kernel(tokens_ref, ids_ref, logits_ref, bins_ref, out_ref):
    tok_rows, width = tokens_ref.shape
    scores = jax.nn.sigmoid(logits_ref[...])
    route_weight = route_scale * scores / jnp.sum(scores, axis=0, keepdims=True)
    bins = bins_ref[...]
    code = ((128 + (bins & 127)) << (bins >> 7)).astype(jnp.float32)
    used = 2 * ids_ref.shape[0] + bins.shape[0]
    tail = jnp.concatenate(
        [
            ids_ref[...].astype(jnp.float32),
            route_weight,
            code,
            jnp.zeros((LANES - used, tok_rows), jnp.float32),
        ],
        axis=0,
    ).astype(jnp.bfloat16)
    row = lax.broadcasted_iota(jnp.int32, (LANES, LANES), 0)
    col = lax.broadcasted_iota(jnp.int32, (LANES, LANES), 1)
    unit = jnp.where(row == col, 1.0, 0.0).astype(jnp.bfloat16)
    turned = lax.dot_general(
        tail, unit, (((0,), (0,)), ((), ())), preferred_element_type=jnp.float32
    )
    out_ref[:, :width] = tokens_ref[...]
    out_ref[:, width:] = turned.astype(jnp.bfloat16)


def pack_rows(tokens, expert_ids, gate_logits, bin_ids):
    tok_rows, width = tokens.shape
    return pl.pallas_call(
        pack_kernel,
        out_shape=jax.ShapeDtypeStruct((tok_rows, width + LANES), jnp.bfloat16),
        name="pack_rows",
    )(
        tokens,
        expert_ids.T,
        gate_logits.T,
        jnp.transpose(bin_ids, (1, 2, 0)).reshape(-1, tok_rows),
    )


def weight_spans(width):
    unit = width // 14
    depths = [unit * n for n in (1, 2, 3, 4)]
    depths.append(width - sum(depths))
    return [(sum(depths[:i]), depth) for i, depth in enumerate(depths)]


def expert_kernel(chosen, blocks, n_parts, me_ref, *refs):
    parts = refs[:n_parts]
    w_ref = refs[n_parts]
    outs = refs[n_parts + 1 : 2 * n_parts + 1]
    code_ref, energy_ref, held, up_ref, sems = refs[2 * n_parts + 1 :]
    width, hidden = w_ref.shape
    tile = min(TILE_N, hidden)
    slices = sems.shape[0]
    spans = weight_spans(width)
    copies = [
        pltpu.make_async_copy(
            w_ref.at[pl.ds(start, depth)], held.at[pl.ds(start, depth)], sems.at[i]
        )
        for i, (start, depth) in enumerate(spans)
    ]
    for copy in copies:
        copy.start()

    tail = jnp.concatenate([p[:, width:] for p in parts], axis=0)
    row = lax.broadcasted_iota(jnp.int32, (LANES, LANES), 0)
    col = lax.broadcasted_iota(jnp.int32, (LANES, LANES), 1)
    bins_at = 2 * chosen
    bins_end = bins_at + chosen * blocks
    choice = jnp.where(col < bins_at, col - chosen, (col - bins_at) // blocks)
    carries = (col >= chosen) & (col < bins_end)
    spread = jnp.where((row == choice) & carries, 1.0, 0.0).astype(jnp.bfloat16)
    ids = jnp.dot(tail, spread, preferred_element_type=jnp.float32)
    lane = lax.broadcasted_iota(jnp.int32, tail.shape, 1)
    mine = (ids == me_ref[0].astype(jnp.float32)) & (lane >= chosen) & (lane < bins_end)
    picked = jnp.where(mine, tail.astype(jnp.float32), 0.0).astype(jnp.bfloat16)
    target = jnp.where(row < bins_at, blocks, (row - bins_at) % blocks)
    usable = (row >= chosen) & (row < bins_end)
    fold = jnp.where((col == target) & usable, 1.0, 0.0).astype(jnp.bfloat16)
    code = jnp.dot(picked, fold, preferred_element_type=jnp.float32)
    code_ref[...] = code
    weight = code[:, blocks : blocks + 1]

    energy = jnp.zeros(energy_ref.shape, jnp.float32)
    unit = lax.broadcasted_iota(jnp.int32, (tile, LANES), 0)
    slot = lax.broadcasted_iota(jnp.int32, (tile, LANES), 1) % blocks
    for i, copy in enumerate(copies):
        copy.wait()
        span = slice(spans[i][0], sum(spans[i]))
        rows = jnp.concatenate([p[:, span] for p in parts], axis=0)
        for j in range(0, hidden, tile):
            up = jnp.dot(rows, held[span, j : j + tile], preferred_element_type=jnp.float32)
            if i > 0:
                up += up_ref[:, j : j + tile]
            if i < slices - 1:
                up_ref[:, j : j + tile] = up
                continue
            mean = jnp.where((unit + j) // BLOCK == slot, 1.0 / BLOCK, 0.0)
            energy += jnp.dot(
                (up * up).astype(jnp.bfloat16),
                mean.astype(jnp.bfloat16),
                preferred_element_type=jnp.float32,
            )
            scaled = (weight * up.astype(jnp.bfloat16).astype(jnp.float32)).astype(jnp.bfloat16)
            at = 0
            for part, out in zip(parts, outs):
                out[:, j : j + tile] = scaled[at : at + part.shape[0]]
                at += part.shape[0]
    energy_ref[...] = energy


def expert_rows(me, parts, weight, chosen, blocks):
    width, hidden = weight.shape
    total = sum(p.shape[0] for p in parts)
    small = jax.ShapeDtypeStruct((total, LANES), jnp.float32)
    inside = pl.BlockSpec(memory_space=pltpu.VMEM)
    return pl.pallas_call(
        functools.partial(expert_kernel, chosen, blocks, len(parts)),
        in_specs=[pl.BlockSpec(memory_space=pltpu.SMEM)]
        + [inside] * len(parts)
        + [pl.BlockSpec(memory_space=pltpu.HBM)],
        out_specs=[inside] * (len(parts) + 2),
        out_shape=[jax.ShapeDtypeStruct((p.shape[0], hidden), jnp.bfloat16) for p in parts]
        + [small, small],
        scratch_shapes=[
            pltpu.VMEM((width, hidden), weight.dtype),
            pltpu.VMEM((total, hidden), jnp.float32),
            pltpu.SemaphoreType.DMA((len(weight_spans(width)),)),
        ],
        compiler_params=pltpu.CompilerParams(vmem_limit_bytes=50 * 1024 * 1024),
        cost_estimate=pl.CostEstimate(
            flops=2 * total * width * hidden,
            bytes_accessed=2 * width * hidden,
            transcendentals=0,
        ),
        name="expert_rows",
    )(me, *parts, weight)


def histogram_kernel(blocks, n_parts, *refs):
    codes, energies = refs[:n_parts], refs[n_parts : 2 * n_parts]
    out_ref = refs[2 * n_parts]
    levels = NBINS // LANES
    row = lax.broadcasted_iota(jnp.int32, (LANES, LANES), 0)
    col = lax.broadcasted_iota(jnp.int32, (LANES, LANES), 1)
    repeat = jnp.where(row == col % blocks, 1.0, 0.0).astype(jnp.bfloat16)
    wide_row = lax.broadcasted_iota(jnp.int32, (LANES, blocks * LANES), 0)
    wide_col = lax.broadcasted_iota(jnp.int32, (LANES, blocks * LANES), 1)
    stretch = jnp.where(wide_row == wide_col // LANES, 1.0, 0.0).astype(jnp.bfloat16)
    total = jnp.zeros((LANES, blocks * LANES), jnp.float32)
    for code_ref, energy_ref in zip(codes, energies):
        code = code_ref[...]
        lane = lax.broadcasted_iota(jnp.int32, code.shape, 1)
        code = jnp.where(lane < blocks, code, 0.0)
        low = code
        high = jnp.where(code > 0.0, 0.0, -1.0)
        for _ in range(levels - 1):
            above = low >= 256.0
            low = jnp.where(above, low * 0.5, low)
            high = jnp.where(above, high + 1.0, high)
        low = jnp.where(code > 0.0, low - 128.0, -1.0)
        high_all = jnp.dot(high.astype(jnp.bfloat16), repeat, preferred_element_type=jnp.float32)
        low_all = jnp.dot(low.astype(jnp.bfloat16), stretch, preferred_element_type=jnp.float32)
        energy = jnp.where(high_all == (lane // blocks).astype(jnp.float32), energy_ref[...], 0.0)
        near = energy.astype(jnp.bfloat16)
        rest = (energy - near.astype(jnp.float32)).astype(jnp.bfloat16)
        spot = lax.broadcasted_iota(jnp.int32, low_all.shape, 1) % LANES
        onehot = jnp.where(low_all == spot.astype(jnp.float32), 1.0, 0.0).astype(jnp.bfloat16)
        for piece in (near, rest):
            total += lax.dot_general(
                piece, onehot, (((0,), (0,)), ((), ())), preferred_element_type=jnp.float32
            )
    pick = lax.broadcasted_iota(jnp.int32, (blocks, LANES), 0)
    for level in range(levels):
        band = total[level * blocks : (level + 1) * blocks]
        line = jnp.zeros((blocks, LANES), jnp.float32)
        for block in range(blocks):
            line = jnp.where(pick == block, band[:, block * LANES : (block + 1) * LANES], line)
        out_ref[:, level * LANES : (level + 1) * LANES] = line


def expert_histogram(codes, energies, blocks):
    rows = sum(c.shape[0] for c in codes)
    return pl.pallas_call(
        functools.partial(histogram_kernel, blocks, len(codes)),
        out_shape=jax.ShapeDtypeStruct((blocks, NBINS), jnp.float32),
        compiler_params=pltpu.CompilerParams(vmem_limit_bytes=24 * 1024 * 1024),
        cost_estimate=pl.CostEstimate(
            flops=4 * rows * LANES * LANES * blocks,
            bytes_accessed=8 * rows * LANES,
            transcendentals=0,
        ),
        name="expert_histogram",
    )(*codes, *energies)


def swap(array, even, odd=None):
    odd = even if odd is None else odd
    size = lax.axis_size("expert")
    return lax.ppermute(array, "expert", [(i, i ^ (odd if i & 1 else even)) for i in range(size)])


def add32(*arrays):
    return functools.reduce(lambda a, b: a + b, [a.astype(jnp.float32) for a in arrays])


def after(array, *others):
    return lax.optimization_barrier((array, *others))[0]


def boxed(packed, me, weight, chosen, blocks):
    far = swap(packed, 16)
    near = swap(packed, 8)
    layers = [packed, near, far, swap(far, 8)]
    halves, others = [], []
    for rows in [packed, near]:
        first = swap(rows, 2, 4)
        second = swap(rows, 4, 2)
        third = swap(first, 4, 2)
        half = jnp.concatenate([rows, first, second, third], axis=0)
        halves.append(half)
        others.append(swap(half, 1))
    fars = jnp.concatenate([far, layers[3]], axis=0)
    first = swap(fars, 2, 4)
    second = swap(fars, 4, 2)
    early = jnp.concatenate([fars, first, second], axis=0)
    early = after(early, others[0])
    early_other = swap(early, 1)
    third = swap(first, 4, 2)
    third_other = swap(third, 1)
    four = len(layers)
    *scaled, code, energy = expert_rows(
        me, halves + [early, third] + others + [early_other, third_other], weight, chosen, blocks
    )
    scaled = [
        *scaled[:2],
        jnp.concatenate(scaled[2:4], axis=0),
        *scaled[4:6],
        jnp.concatenate(scaled[6:8], axis=0),
    ]
    tok_rows = packed.shape[0]

    def by_layer(parts):
        near_two = jnp.stack(parts[:2]).reshape(2, 4, tok_rows, -1)
        far_two = jnp.swapaxes(parts[2].reshape(4, 2, tok_rows, -1), 0, 1)
        return jnp.concatenate([near_two, far_two], axis=0)

    keep, send = by_layer(scaled[:3]), by_layer(scaled[3:])
    cross = add32(keep[:, 3], swap(send[:, 3], 1)).astype(jnp.bfloat16)
    came = swap(send[:, :3], 1)
    leaving = add32(keep[:, 1:3], came[:, 1:]).astype(jnp.bfloat16)
    partial = add32(
        keep[:, 0],
        came[:, 0],
        swap(cross, 6),
        swap(leaving[:, 0], 2, 4),
        swap(leaving[:, 1], 4, 2),
    )
    histogram = expert_histogram([code], [energy], blocks)
    partial = after(partial, histogram)
    home = [swap(partial[i].astype(jnp.bfloat16), 8 * i) for i in range(1, four)]
    mixed = add32(partial[0], *home).astype(jnp.bfloat16)
    return mixed, histogram


def plain(packed, me, weight, chosen, blocks):
    rows = lax.all_gather(packed, "expert", axis=0, tiled=True)
    step = LANES if rows.shape[0] % LANES == 0 else packed.shape[0]
    scaled, codes, energies = [], [], []
    for at in range(0, rows.shape[0], step):
        part, code, energy = expert_rows(me, [rows[at : at + step]], weight, chosen, blocks)
        scaled.append(part)
        codes.append(code)
        energies.append(energy)
    mixed = lax.psum_scatter(
        jnp.concatenate(scaled, axis=0).astype(jnp.float32),
        "expert",
        scatter_dimension=0,
        tiled=True,
    )
    return mixed.astype(jnp.bfloat16), expert_histogram(codes, energies, blocks)


def shards(tokens, expert_ids, gate_logits, bin_ids, up_weight):
    chosen, blocks = bin_ids.shape[1:]
    packed = pack_rows(tokens, expert_ids, gate_logits, bin_ids)
    me = lax.axis_index("expert").astype(jnp.int32)[None]
    weight = lax.all_gather(up_weight, "fsdp", axis=1, tiled=True)[0]
    route = boxed if lax.axis_size("expert") == 32 else plain
    mixed, histogram = route(packed, me, weight, chosen, blocks)
    histogram = lax.psum_scatter(histogram[None], "fsdp", scatter_dimension=2, tiled=True)
    return mixed, histogram


def solution(mesh):
    return jax.shard_map(
        shards,
        mesh=mesh,
        in_specs=(
            P(("rep", "expert", "fsdp"), None),
            P(("rep", "expert", "fsdp"), None),
            P(("rep", "expert", "fsdp"), None),
            P(("rep", "expert", "fsdp"), None, None),
            P("expert", "fsdp", None),
        ),
        out_specs=(P(("rep", "expert", "fsdp"), None), P(("rep", "expert"), None, "fsdp")),
        check_vma=False,
    )
```
